32 devices in a mesh: section: 2 (over x), clip: 4 (over y, core), seq: 4 (over z).
Axes of the slice: x: 2, y: 2, z: 4, core: 2. Of those that a mesh axis runs over, the one named last changes fastest.
Arguments:
- ends_in: bfloat16 [2, 2, 4, 256, 768], P('section', None, 'clip', 'seq'), may hold values from -6 to 6
- clip_counts: int32 [2], replicated, may hold values from 1 to 4, as said below
- qkv_weight: bfloat16 [2, 768, 2304], P('section', ('clip', 'seq')), may hold values from -0.21875 to 0.21875
- out_weight: bfloat16 [2, 768, 768], P('section', ('clip', 'seq')), may hold values from -0.875 to 0.875
- up_weight: bfloat16 [2, 768, 3072], P('section', ('clip', 'seq')), may hold values from -0.21875 to 0.21875
- down_weight: bfloat16 [2, 3072, 768], P('section', ('clip', 'seq')), may hold values from -0.109375 to 0.109375
- norm_gains: bfloat16 [2, 2, 768], P('section', None, ('clip', 'seq')), may hold values from 0.099609375 to 1.8984375
- vec_bias: bfloat16 [2, 6, 768], P('section', None, ('clip', 'seq')), may hold values from -2 to 2
- up_bias: bfloat16 [2, 3072], P('section', ('clip', 'seq')), may hold values from -2 to 2
Outputs:
- ends_out: float32 [2, 2, 4, 256, 768], P('section', None, 'clip', 'seq')
- qkv_grad: float32 [2, 768, 2304], P('section', ('clip', 'seq'))
- out_grad: float32 [2, 768, 768], P('section', ('clip', 'seq'))
- up_grad: float32 [2, 768, 3072], P('section', ('clip', 'seq'))
- down_grad: float32 [2, 3072, 768], P('section', ('clip', 'seq'))
- gains_grad: float32 [2, 2, 768], P('section', None, ('clip', 'seq'))
- bias_grad: float32 [2, 6, 768], P('section', None, ('clip', 'seq'))
- up_bias_grad: float32 [2, 3072], P('section', ('clip', 'seq'))
The draws below stay inside these ranges and needn't reach their ends.
Inputs may be any that keep to these rules, and one draw needn't show every extreme that they name: clip_counts is 4 for every micro-batch but one, which holds fewer valid clips: its first clip_counts[m] slots.
All inputs are finite; a program needn't handle non-finite values.
Results may differ from the reference program's by a relative error of at most 0.017.
Values may be sent and summed in bfloat16 or wider, within the bound.
A program may use at most 192 MiB of HBM per device.

```python
import jax
import jax.numpy as jnp
from jax import lax

D = 768
FF = 3072
HEADS = 12
HEAD_DIM = 64
MB = 2
SECTIONS = 2
CLIPS = 4
LENGTH = 256


def draw_clip_counts(key, part):
    key = jax.random.fold_in(key, 7)
    pick_key, count_key = jax.random.split(key)
    short_index = jax.random.randint(pick_key, (), 0, MB).astype(jnp.int32)
    short_count = jax.random.randint(count_key, (), 1, CLIPS).astype(jnp.int32)
    positions = jnp.arange(MB, dtype=jnp.int32)
    return jnp.where(positions == short_index, short_count, jnp.int32(CLIPS)).astype(jnp.int32)


def block_scale(own_key, shape, cuts, least, high):
    level, own = 1.0, jax.random.fold_in(own_key, 6)
    for position, blocks in cuts:
        draws = jnp.exp(jax.random.uniform(jax.random.fold_in(own, position), (blocks,), jnp.float32, least / len(cuts), high / len(cuts)))
        level = level * jnp.repeat(draws, shape[position] // blocks).reshape([-1 if axis == position else 1 for axis in range(len(shape))])
    return level


def scatter_about(rng, extent, width, limit, pieces=(), held_as=jnp.bfloat16):
    result = width * jax.random.normal(rng, extent, jnp.float32)
    if pieces:
        result = result * block_scale(rng, extent, pieces, -0.22, 0.18)
    return jnp.clip(result, -limit, limit).astype(held_as)


def setup_inputs(seed: int = 0) -> dict:
    arg_keys = jax.random.split(jax.random.key(seed), 10)
    return {
        "ends_in": scatter_about(arg_keys[0], (SECTIONS, MB, CLIPS, LENGTH, D), 1.0, 6.0, ((0, 2), (2, 4), (3, 4))),
        "clip_counts": draw_clip_counts(jax.random.fold_in(arg_keys[9], 71), 0),
        "qkv_weight": scatter_about(arg_keys[2], (SECTIONS, D, 3 * D), D ** -0.5, 0.21875, ((0, 2), (1, 16))),
        "out_weight": scatter_about(arg_keys[3], (SECTIONS, D, D), (D // 16) ** -0.5, 0.875, ((0, 2), (1, 16))),
        "up_weight": scatter_about(arg_keys[4], (SECTIONS, D, FF), D ** -0.5, 0.21875, ((0, 2), (1, 16))),
        "down_weight": scatter_about(arg_keys[5], (SECTIONS, FF, D), FF ** -0.5, 0.109375, ((0, 2), (1, 16))),
        "norm_gains": jnp.clip(1.0 + 0.18 * jax.random.normal(arg_keys[6], (SECTIONS, 2, D), jnp.float32), 0.099609375, 1.8984375).astype(jnp.bfloat16),
        "vec_bias": scatter_about(arg_keys[7], (SECTIONS, 6, D), 0.3, 2.0, ((0, 2), (2, 16))),
        "up_bias": scatter_about(arg_keys[8], (SECTIONS, FF), 0.3, 2.0, ((0, 2), (1, 16))),
    }


@jax.custom_vjp
def low(v):
    return lax.optimization_barrier(v.astype(jnp.bfloat16)).astype(jnp.float32)

@jax.custom_vjp
def low_back(v):
    return v

def low_keep(v):
    return (low(v), None)

def low_pass(kept, grad):
    return (grad,)

def back_keep(v):
    return (v, None)

def back_low(kept, grad):
    return (low(grad),)
low.defvjp(low_keep, low_pass)
low_back.defvjp(back_keep, back_low)

def product(left, right):
    return jnp.einsum('nld,de->nle', left, right, precision=lax.Precision.HIGHEST)

def layer_norm(values, gain_row, shift_row):
    centered = values - lax.optimization_barrier(jnp.mean(values, axis=-1, keepdims=True))
    inverse = lax.rsqrt(lax.optimization_barrier(jnp.mean(centered * centered, axis=-1, keepdims=True)) + 1e-05)
    return centered * inverse * gain_row + shift_row

def attend(triple):
    query_rows, key_rows, value_rows = triple
    query_heads = query_rows.reshape(LENGTH, HEADS, HEAD_DIM)
    key_heads = key_rows.reshape(LENGTH, HEADS, HEAD_DIM)
    value_heads = value_rows.reshape(LENGTH, HEADS, HEAD_DIM)
    scores = jnp.einsum('qhd,khd->hqk', query_heads, key_heads, precision=lax.Precision.HIGHEST)
    scores = low_back(scores * HEAD_DIM ** (-0.5))
    soft_probs = low(jax.nn.softmax(scores, axis=-1))
    mixed_rows = jnp.einsum('hqk,khd->qhd', soft_probs, value_heads, precision=lax.Precision.HIGHEST)
    return mixed_rows.reshape(LENGTH, D)

def encoder_layer(inputs, qkv_weight, out_weight, up_weight, down_weight, gain_rows, shifts, up_shift):
    normed_one = low(layer_norm(inputs, gain_rows[0], shifts[0]))
    projected = product(normed_one, qkv_weight)
    query_rows = low(low_back(projected[..., :D] + shifts[2]))
    key_rows = low(low_back(projected[..., D:2 * D]))
    value_rows = low(low_back(projected[..., 2 * D:] + shifts[3]))
    mixed_rows = lax.map(jax.checkpoint(attend), (query_rows, key_rows, value_rows))
    mixed_rows = low(low_back(mixed_rows))
    hidden = inputs + low_back(product(mixed_rows, out_weight) + shifts[4])
    normed_two = low(layer_norm(hidden, gain_rows[1], shifts[1]))
    before = low_back(product(normed_two, up_weight) + up_shift)
    activated = low(jax.nn.gelu(before, approximate=False))
    return hidden + low_back(product(activated, down_weight) + shifts[5])

def reference(ends_in, clip_counts, qkv_weight, out_weight, up_weight, down_weight, norm_gains, vec_bias, up_bias):
    start = ends_in[0].astype(jnp.float32).reshape(MB * CLIPS, LENGTH, D)
    valid_rows = (jnp.arange(CLIPS)[None, :] < clip_counts[:, None]).astype(jnp.float32)
    cotangent = ends_in[1].astype(jnp.float32) * valid_rows[:, :, None, None]
    cotangent = cotangent.reshape(MB * CLIPS, LENGTH, D)
    params = tuple((weight_set.astype(jnp.float32) for weight_set in (qkv_weight, out_weight, up_weight, down_weight, norm_gains, vec_bias, up_bias)))

    def stacked(inputs, *weight_sets):
        hidden = inputs
        for section_index in range(SECTIONS):
            hidden = encoder_layer(hidden, *(weight_set[section_index] for weight_set in weight_sets))
            if section_index + 1 < SECTIONS:
                hidden = low(low_back(hidden))
        return hidden
    output, pull = jax.vjp(stacked, start, *params)
    grads = pull(cotangent)
    shape_out = (MB, CLIPS, LENGTH, D)
    ends_out = jnp.stack([grads[0].reshape(shape_out), output.reshape(shape_out)])
    return (ends_out, grads[1], grads[2], grads[3], grads[4], grads[5], grads[6], grads[7])
```

```python
import jax
import jax.numpy as jnp
from jax import lax
from jax.sharding import Mesh
from jax.sharding import PartitionSpec as P

HEAD_DIM = 64
SCALE = HEAD_DIM ** (-0.5)


def norm_parts(values):
    centered = values - jnp.mean(values, axis=-1, keepdims=True)
    inverse = lax.rsqrt(jnp.mean(centered * centered, axis=-1, keepdims=True) + 1e-05)
    return centered * inverse, inverse


def norm_back(grad_hat, normal, inverse):
    first_term = grad_hat - jnp.mean(grad_hat, axis=-1, keepdims=True)
    return inverse * (first_term - normal * jnp.mean(grad_hat * normal, axis=-1, keepdims=True))


def matmul(left, right):
    return jnp.dot(left, right, preferred_element_type=jnp.float32)


def times_transposed(left, right):
    return lax.dot_general(
        left, right, (((1,), (1,)), ((), ())), preferred_element_type=jnp.float32
    )


def transposed_times(left, right):
    return lax.dot_general(
        left, right, (((0,), (0,)), ((), ())), preferred_element_type=jnp.float32
    )


def product(spec, left, right):
    return jnp.einsum(spec, left, right, preferred_element_type=jnp.float32)


def to_heads(rows, groups, clips, frames):
    peers = lax.axis_size("seq")
    own = rows.shape[1] // (groups * peers)
    parts = rows.reshape(clips, frames, groups, peers, own).transpose(3, 2, 0, 1, 4)
    got = lax.all_to_all(parts, "seq", 0, 0)
    got = got.transpose(1, 2, 0, 3, 4).reshape(groups, clips, peers * frames, own)
    return got.reshape(groups, clips, peers * frames, own // HEAD_DIM, HEAD_DIM)


def from_heads(heads, groups, clips, frames):
    peers = lax.axis_size("seq")
    own = heads.shape[-1]
    parts = heads.reshape(groups, clips, peers, frames, own).transpose(2, 0, 1, 3, 4)
    got = lax.all_to_all(parts, "seq", 0, 0)
    return got.transpose(2, 3, 1, 0, 4).reshape(clips * frames, groups * peers * own)


def layer_forward(row_data, clips, frames, weights):
    qkv_weight, out_weight, up_weight, down_weight, gain_rows, shifts, up_shift = weights
    width = row_data.shape[1]
    normal_one, inverse_one = norm_parts(row_data)
    normed_one = (normal_one * gain_rows[0] + shifts[0]).astype(jnp.bfloat16)
    qkv_shift = jnp.concatenate([shifts[2], jnp.zeros_like(shifts[2]), shifts[3]])
    projected = (matmul(normed_one, qkv_weight) + qkv_shift).astype(jnp.bfloat16)
    triple = to_heads(projected, 3, clips, frames)
    scores = product("nqhd,nkhd->nhqk", triple[0], triple[1]) * SCALE
    weights_exp = jnp.exp(scores - jnp.max(scores, axis=-1, keepdims=True))
    soft = weights_exp / jnp.sum(weights_exp, axis=-1, keepdims=True)
    probs = soft.astype(jnp.bfloat16)
    mixed_heads = product("nhqk,nkhd->nqhd", probs, triple[2]).astype(jnp.bfloat16)
    total = mixed_heads.shape[1]
    mixed_rows = from_heads(mixed_heads.reshape(1, clips, total, -1), 1, clips, frames)
    hidden = row_data + matmul(mixed_rows, out_weight) + shifts[4]
    normal_two, inverse_two = norm_parts(hidden)
    normed_two = (normal_two * gain_rows[1] + shifts[1]).astype(jnp.bfloat16)
    before = matmul(normed_two, up_weight) + up_shift
    half = 0.5 * (1.0 + lax.erf(before * (0.5**0.5)))
    activated = (before * half).astype(jnp.bfloat16)
    slope = half + before * jnp.exp(-0.5 * before * before) * 0.3989422804014327
    result = hidden + matmul(activated, down_weight) + shifts[5]
    kept = (
        normal_one,
        inverse_one,
        normed_one,
        triple,
        soft,
        probs,
        mixed_rows,
        normal_two,
        inverse_two,
        normed_two,
        slope,
        activated,
    )
    return result, kept


def layer_backward(grad_rows, clips, frames, kept, weights):
    qkv_weight, out_weight, up_weight, down_weight, gain_rows, shifts, up_shift = weights
    (
        normal_one,
        inverse_one,
        normed_one,
        triple,
        soft,
        probs,
        mixed_rows,
        normal_two,
        inverse_two,
        normed_two,
        slope,
        activated,
    ) = kept
    down_g = grad_rows.astype(jnp.bfloat16)
    up_g = (times_transposed(down_g, down_weight) * slope).astype(jnp.bfloat16)
    norm_two_g = times_transposed(up_g, up_weight)
    hidden_g = grad_rows + norm_back(norm_two_g * gain_rows[1], normal_two, inverse_two)
    branch_g = hidden_g.astype(jnp.bfloat16)
    mixed_g = times_transposed(branch_g, out_weight).astype(jnp.bfloat16)
    mixed_heads = to_heads(mixed_g, 1, clips, frames)[0]
    probs_g = product("nqhd,nkhd->nhqk", mixed_heads, triple[2])
    delta = jnp.sum(soft * probs_g, axis=-1, keepdims=True)
    scores_g = (soft * (probs_g - delta)).astype(jnp.bfloat16)
    query_g = product("nhqk,nkhd->nqhd", scores_g, triple[1]) * SCALE
    key_g = product("nhqk,nqhd->nkhd", scores_g, triple[0]) * SCALE
    value_g = product("nhqk,nqhd->nkhd", probs, mixed_heads)
    stacked = jnp.stack([query_g, key_g, value_g]).astype(jnp.bfloat16)
    total = stacked.shape[2]
    qkv_g = from_heads(stacked.reshape(3, clips, total, -1), 3, clips, frames)
    norm_one_g = times_transposed(qkv_g, qkv_weight)
    input_g = hidden_g + norm_back(norm_one_g * gain_rows[0], normal_one, inverse_one)
    operands = (normed_one, qkv_g, mixed_rows, branch_g, normed_two, up_g, activated, down_g)
    sums = [
        jnp.sum(norm_one_g * normal_one, axis=0),
        jnp.sum(norm_two_g * normal_two, axis=0),
        jnp.sum(norm_one_g, axis=0),
        jnp.sum(norm_two_g, axis=0),
    ]
    return input_g, operands, sums


def gather(shard):
    pairs = lax.axis_size("pair")
    own = lax.all_gather(shard, ("pair", "seq"), axis=0, tiled=True)
    own = own.reshape(pairs, own.shape[0] // pairs, own.shape[1])
    both = lax.all_gather(own, "core", axis=1, tiled=False)
    return both.reshape(-1, shard.shape[1])


def my_half(columns):
    pairs = lax.axis_size("pair")
    rows, width = columns.shape
    view = columns.reshape(rows, pairs, 2, width // (2 * pairs))
    mine = lax.dynamic_index_in_dim(view, lax.axis_index("core"), 2, keepdims=False)
    return mine.reshape(rows, width // 2)


def on_device(
    ends_in, clip_counts, qkv_weight, out_weight, up_weight, down_weight, norm_gains, vec_bias, up_bias
):
    ends_local = ends_in[0]
    batches, local_clips, frames, width = ends_local.shape
    clips = batches * local_clips
    rows = clips * frames
    owners = lax.axis_size("pair") * 2 * lax.axis_size("seq")
    share = width // owners
    ff_share = up_bias.shape[1]
    small = jnp.concatenate([norm_gains[0], vec_bias[0]], axis=0).reshape(-1)
    small = jnp.concatenate([small, up_bias[0]])
    extra = -(-small.shape[0] // width)
    extra_rows = -(-extra // 16) * 16
    small = jnp.pad(small, (0, extra_rows * width - small.shape[0])).reshape(extra_rows, width)
    out_small = gather(jnp.concatenate([out_weight[0], small], axis=0))
    out_small = out_small.reshape(owners, share + extra_rows, width)
    out_full = out_small[:, :share].reshape(width, width)
    small_full = out_small[:, share:].reshape(owners, extra_rows * width).astype(jnp.float32)
    rows8 = small_full[:, : 8 * share].reshape(owners, 8, share)
    rows8 = rows8.transpose(1, 0, 2).reshape(8, width)
    up_shift = small_full[:, 8 * share : 8 * share + ff_share].reshape(-1)
    weights = (
        gather(qkv_weight[0]),
        out_full,
        gather(up_weight[0]),
        gather(down_weight[0]),
        rows8[:2],
        rows8[2:],
        up_shift,
    )
    first = lax.axis_index("section") == 0
    ends_rows = ends_local.reshape(rows, width)
    passed, _ = layer_forward(ends_rows.astype(jnp.float32), clips, frames, weights)
    link = lax.ppermute(passed.astype(jnp.bfloat16), "section", [(0, 1)])
    layer_in = jnp.where(first, ends_rows, link).astype(jnp.float32)
    top, kept = layer_forward(layer_in, clips, frames, weights)

    clip_ids = (lax.axis_index("pair") * 2 + lax.axis_index("core")) * local_clips
    clip_ids = clip_ids + jnp.arange(local_clips, dtype=jnp.int32)
    valid = (clip_ids[None, :] < clip_counts[:, None]).astype(jnp.bfloat16)
    cotangent = (ends_local * valid[:, :, None, None]).reshape(rows, width)
    passed_g, _, _ = layer_backward(
        cotangent.astype(jnp.float32), clips, frames, kept, weights
    )
    link_g = lax.ppermute(passed_g.astype(jnp.bfloat16), "section", [(1, 0)])
    grad_in = jnp.where(first, link_g, cotangent).astype(jnp.float32)
    bottom, operands, sums = layer_backward(grad_in, clips, frames, kept, weights)

    def over_rows(index):
        return jnp.sum(operands[index], axis=0, dtype=jnp.float32)

    qkv_sum = over_rows(1)
    columns = jnp.stack(
        sums + [qkv_sum[:width], qkv_sum[2 * width :], over_rows(3), over_rows(7)]
    )
    small_g = jnp.concatenate(
        [
            columns.reshape(8, owners, share).transpose(1, 0, 2).reshape(owners, 8 * share),
            over_rows(5).reshape(owners, ff_share),
        ],
        axis=1,
    )
    spare = extra_rows * width - small_g.shape[1]
    small_g = jnp.pad(small_g, ((0, 0), (0, spare))).reshape(owners * extra_rows, width)
    small_half = lax.psum_scatter(
        small_g.reshape(lax.axis_size("pair"), 2, -1, width),
        "core",
        scatter_dimension=1,
        tiled=False,
    ).reshape(owners // 2, extra_rows, width)

    def share_grad(left, right, more=None):
        both_left = lax.all_gather(left, "core", axis=0, tiled=True)
        both_right = lax.all_gather(right, "core", axis=0, tiled=True)
        part = transposed_times(my_half(both_left), both_right).astype(jnp.bfloat16)
        if more is not None:
            part = part.reshape(owners // 2, -1, part.shape[1])
            part = jnp.concatenate([part, more.astype(jnp.bfloat16)], axis=1)
            part = part.reshape(-1, part.shape[2])
        return lax.psum_scatter(
            part, ("pair", "seq"), scatter_dimension=0, tiled=True
        ).astype(jnp.float32)

    down_part = share_grad(operands[6], operands[7])
    up_part = share_grad(operands[4], operands[5])
    out_part = share_grad(operands[2], operands[3], small_half)
    qkv_part = share_grad(operands[0], operands[1])
    small_part = out_part[share:].reshape(-1)
    rows_part = small_part[: 8 * share].reshape(8, share)
    ends_out = jnp.where(first, bottom, top).reshape(1, batches, local_clips, frames, width)
    return (
        ends_out,
        qkv_part[None],
        out_part[:share][None],
        up_part[None],
        down_part[None],
        rows_part[None, :2],
        rows_part[None, 2:],
        small_part[None, 8 * share : 8 * share + ff_share],
    )


def solution(mesh):
    sections, clips, seqs = mesh.devices.shape
    fine = Mesh(
        mesh.devices.reshape(sections, clips // 2, 2, seqs), ("section", "pair", "core", "seq")
    )
    spread = ("pair", "core", "seq")
    ends = P("section", None, ("pair", "core"), "seq", None)
    rowed = P("section", spread, None)
    lanes = P("section", None, spread)
    up_bias = P("section", spread)
    return jax.shard_map(
        on_device,
        mesh=fine,
        in_specs=(ends, P(), rowed, rowed, rowed, rowed, lanes, lanes, up_bias),
        out_specs=(ends, rowed, rowed, rowed, rowed, lanes, lanes, up_bias),
        check_vma=False,
    )
```

```python
import functools

import jax
import jax.numpy as jnp
from jax import lax
from jax.experimental import pallas as pl
from jax.experimental.pallas import tpu as pltpu
from jax.sharding import Mesh
from jax.sharding import PartitionSpec as P

HEAD_DIM = 64
SCALE = HEAD_DIM ** (-0.5)


def norm_parts(values):
    centered = values - jnp.mean(values, axis=-1, keepdims=True)
    inverse = lax.rsqrt(jnp.mean(centered * centered, axis=-1, keepdims=True) + 1e-05)
    return centered * inverse, inverse


def norm_back(grad_hat, normal, inverse):
    first_term = grad_hat - jnp.mean(grad_hat, axis=-1, keepdims=True)
    return inverse * (first_term - normal * jnp.mean(grad_hat * normal, axis=-1, keepdims=True))


def matmul(left, right):
    return jnp.dot(left, right, preferred_element_type=jnp.float32)


def times_transposed(left, right):
    return lax.dot_general(
        left, right, (((1,), (1,)), ((), ())), preferred_element_type=jnp.float32
    )


def transposed_times(left, right):
    return lax.dot_general(
        left, right, (((0,), (0,)), ((), ())), preferred_element_type=jnp.float32
    )


def product(spec, left, right):
    return jnp.einsum(spec, left, right, preferred_element_type=jnp.float32)


def to_heads(rows, groups, clips, frames):
    peers = lax.axis_size("seq")
    own = rows.shape[1] // (groups * peers)
    parts = rows.reshape(clips, frames, groups, peers, own).transpose(3, 2, 0, 1, 4)
    got = lax.all_to_all(parts, "seq", 0, 0)
    got = got.transpose(1, 2, 0, 3, 4).reshape(groups, clips, peers * frames, own)
    return got.reshape(groups, clips, peers * frames, own // HEAD_DIM, HEAD_DIM)


def from_heads(heads, groups, clips, frames):
    peers = lax.axis_size("seq")
    own = heads.shape[-1]
    parts = heads.reshape(groups, clips, peers, frames, own).transpose(2, 0, 1, 3, 4)
    got = lax.all_to_all(parts, "seq", 0, 0)
    return got.transpose(2, 3, 1, 0, 4).reshape(clips * frames, groups * peers * own)


def layer_forward(row_data, clips, frames, weights):
    qkv_weight, out_weight, up_weight, down_weight, gain_rows, shifts, up_shift = weights
    width = row_data.shape[1]
    normal_one, inverse_one = norm_parts(row_data)
    normed_one = (normal_one * gain_rows[0] + shifts[0]).astype(jnp.bfloat16)
    qkv_shift = jnp.concatenate([shifts[2], jnp.zeros_like(shifts[2]), shifts[3]])
    projected = (matmul(normed_one, qkv_weight) + qkv_shift).astype(jnp.bfloat16)
    triple = to_heads(projected, 3, clips, frames)
    scores = product("nqhd,nkhd->nhqk", triple[0], triple[1]) * SCALE
    weights_exp = jnp.exp(scores - jnp.max(scores, axis=-1, keepdims=True))
    soft = weights_exp / jnp.sum(weights_exp, axis=-1, keepdims=True)
    probs = soft.astype(jnp.bfloat16)
    mixed_heads = product("nhqk,nkhd->nqhd", probs, triple[2]).astype(jnp.bfloat16)
    total = mixed_heads.shape[1]
    mixed_rows = from_heads(mixed_heads.reshape(1, clips, total, -1), 1, clips, frames)
    hidden = row_data + matmul(mixed_rows, out_weight) + shifts[4]
    normal_two, inverse_two = norm_parts(hidden)
    normed_two = (normal_two * gain_rows[1] + shifts[1]).astype(jnp.bfloat16)
    before = matmul(normed_two, up_weight) + up_shift
    half = 0.5 * (1.0 + lax.erf(before * (0.5**0.5)))
    activated = (before * half).astype(jnp.bfloat16)
    slope = half + before * jnp.exp(-0.5 * before * before) * 0.3989422804014327
    result = hidden + matmul(activated, down_weight) + shifts[5]
    kept = (
        normal_one,
        inverse_one,
        normed_one,
        triple,
        soft,
        probs,
        mixed_rows,
        normal_two,
        inverse_two,
        normed_two,
        slope,
        activated,
    )
    return result, kept


def layer_backward(grad_rows, clips, frames, kept, weights):
    qkv_weight, out_weight, up_weight, down_weight, gain_rows, shifts, up_shift = weights
    (
        normal_one,
        inverse_one,
        normed_one,
        triple,
        soft,
        probs,
        mixed_rows,
        normal_two,
        inverse_two,
        normed_two,
        slope,
        activated,
    ) = kept
    down_g = grad_rows.astype(jnp.bfloat16)
    up_g = (times_transposed(down_g, down_weight) * slope).astype(jnp.bfloat16)
    norm_two_g = times_transposed(up_g, up_weight)
    hidden_g = grad_rows + norm_back(norm_two_g * gain_rows[1], normal_two, inverse_two)
    branch_g = hidden_g.astype(jnp.bfloat16)
    mixed_g = times_transposed(branch_g, out_weight).astype(jnp.bfloat16)
    mixed_heads = to_heads(mixed_g, 1, clips, frames)[0]
    probs_g = product("nqhd,nkhd->nhqk", mixed_heads, triple[2])
    delta = jnp.sum(soft * probs_g, axis=-1, keepdims=True)
    scores_g = (soft * (probs_g - delta)).astype(jnp.bfloat16)
    query_g = product("nhqk,nkhd->nqhd", scores_g, triple[1]) * SCALE
    key_g = product("nhqk,nqhd->nkhd", scores_g, triple[0]) * SCALE
    value_g = product("nhqk,nqhd->nkhd", probs, mixed_heads)
    stacked = jnp.stack([query_g, key_g, value_g]).astype(jnp.bfloat16)
    total = stacked.shape[2]
    qkv_g = from_heads(stacked.reshape(3, clips, total, -1), 3, clips, frames)
    norm_one_g = times_transposed(qkv_g, qkv_weight)
    input_g = hidden_g + norm_back(norm_one_g * gain_rows[0], normal_one, inverse_one)
    operands = (normed_one, qkv_g, mixed_rows, branch_g, normed_two, up_g, activated, down_g)
    sums = [
        jnp.sum(norm_one_g * normal_one, axis=0),
        jnp.sum(norm_two_g * normal_two, axis=0),
        jnp.sum(norm_one_g, axis=0),
        jnp.sum(norm_two_g, axis=0),
    ]
    return input_g, operands, sums


def turn(axis, step):
    size = lax.axis_size(axis)
    return lax.rem(lax.axis_index(axis) + step, size)


def offsets(size):
    near = []
    for step in range(1, size // 2 + 1):
        near.append(step)
        if size - step != step:
            near.append(size - step)
    return near


def meet(partners):
    barrier = pltpu.get_barrier_semaphore()
    for partner in partners:
        pl.semaphore_signal(
            barrier, inc=1, device_id=partner, device_id_type=pl.DeviceIdType.MESH
        )
    pl.semaphore_wait(barrier, len(partners))


def remote(source, target, send, receive, device):
    return pltpu.make_async_remote_copy(
        src_ref=source,
        dst_ref=target,
        send_sem=send,
        recv_sem=receive,
        device_id=device,
        device_id_type=pl.DeviceIdType.MESH,
    )


def gather_kernel(pairs, seqs, count, *refs):
    shards, fulls = refs[:count], refs[count : 2 * count]
    own_sem, seq_send, pair_send, core_send, lane_recv, core_recv = refs[2 * count :]
    pair, core, seq = (lax.axis_index(name) for name in ("pair", "core", "seq"))
    other = {"core": 1 - core}
    seq_steps, pair_steps = offsets(seqs), offsets(pairs)
    meet(
        [{"seq": turn("seq", step)} for step in seq_steps]
        + [{"pair": turn("pair", step)} for step in pair_steps]
        + [other]
    )

    def slot(pair_index, core_index, seq_index):
        return (pair_index * 2 + core_index) * seqs + seq_index

    started, waits = [], []

    def start(copy):
        copy.start()
        started.append(copy)

    def to_core(w, source, place, index):
        start(
            remote(
                source, fulls[w].at[place], core_send.at[w, index], core_recv.at[w, index], other
            )
        )

    def to_pairs(w, source, place, seq_step):
        for step in pair_steps:
            index = step * seqs + seq_step
            start(
                remote(
                    source,
                    fulls[w].at[place],
                    pair_send.at[w, index],
                    lane_recv.at[w, index],
                    {"pair": turn("pair", step)},
                )
            )

    mine = slot(pair, core, seq)
    local = []
    for w in range(count):
        for step in seq_steps:
            start(
                remote(
                    shards[w],
                    fulls[w].at[mine],
                    seq_send.at[w, step],
                    lane_recv.at[w, step],
                    {"seq": turn("seq", step)},
                )
            )
        to_pairs(w, shards[w], mine, 0)
        to_core(w, shards[w], mine, 0)
        copy = pltpu.make_async_copy(shards[w], fulls[w].at[mine], own_sem.at[w])
        copy.start()
        local.append(copy)

    def arrived(w, place, index, semaphores):
        there = fulls[w].at[place]
        remote(there, there, core_send.at[w, index], semaphores.at[w, index], other).wait_recv()

    for w in range(count):
        for step in seq_steps:
            place = slot(pair, core, turn("seq", seqs - step))
            arrived(w, place, step, lane_recv)
            to_pairs(w, fulls[w].at[place], place, step)
            to_core(w, fulls[w].at[place], place, step)
        for seq_step in [0] + seq_steps:
            for step in pair_steps:
                place = slot(
                    turn("pair", pairs - step), core, turn("seq", seqs - seq_step)
                )
                index = step * seqs + seq_step
                arrived(w, place, index, lane_recv)
                to_core(w, fulls[w].at[place], place, index)
    for w in range(count):
        for seq_step in range(seqs):
            for step in range(pairs):
                place = slot(
                    turn("pair", pairs - step), 1 - core, turn("seq", seqs - seq_step)
                )
                arrived(w, place, step * seqs + seq_step, core_recv)
    for copy in started:
        copy.wait_send()
    for copy in local:
        copy.wait()


def gather_all(shards):
    pairs, seqs = lax.axis_size("pair"), lax.axis_size("seq")
    count, lanes = len(shards), pairs * seqs
    dma = pltpu.SemaphoreType.DMA
    anywhere = pl.BlockSpec(memory_space=pl.ANY)
    return pl.pallas_call(
        functools.partial(gather_kernel, pairs, seqs, count),
        out_shape=[jax.ShapeDtypeStruct((2 * lanes,) + x.shape, x.dtype) for x in shards],
        in_specs=[anywhere] * count,
        out_specs=[anywhere] * count,
        scratch_shapes=[
            dma((count,)),
            dma((count, seqs)),
            dma((count, lanes)),
            dma((count, lanes)),
            dma((count, lanes)),
            dma((count, lanes)),
        ],
        compiler_params=pltpu.CompilerParams(collective_id=0, has_side_effects=True),
        name="gather_weights",
    )(*shards)


def swap_kernel(count, *refs):
    sources, targets = refs[:count], refs[count : 2 * count]
    send, receive = refs[2 * count :]
    other = {"core": 1 - lax.axis_index("core")}
    meet([other])
    copies = [
        remote(sources[i], targets[i], send.at[i], receive.at[i], other) for i in range(count)
    ]
    for copy in copies:
        copy.start()
    for copy in copies:
        copy.wait()


def swap_cores(arrays):
    count = len(arrays)
    vmem = pl.BlockSpec(memory_space=pltpu.VMEM)
    return pl.pallas_call(
        functools.partial(swap_kernel, count),
        out_shape=[jax.ShapeDtypeStruct(x.shape, x.dtype) for x in arrays],
        in_specs=[vmem] * count,
        out_specs=[vmem] * count,
        scratch_shapes=[pltpu.SemaphoreType.DMA((count,)), pltpu.SemaphoreType.DMA((count,))],
        compiler_params=pltpu.CompilerParams(
            collective_id=1, has_side_effects=True, vmem_limit_bytes=24 * 2**20
        ),
        name="swap_cores",
    )(*arrays)


def scatter_kernel(pairs, seqs, count, *refs):
    parts, outs = refs[:count], refs[count : 2 * count]
    pair_in = refs[2 * count : 3 * count]
    seq_out = refs[3 * count : 4 * count]
    seq_in = refs[4 * count : 5 * count]
    pair_send, pair_recv, seq_send, seq_recv = refs[5 * count :]
    pair = lax.axis_index("pair")
    seq_steps, pair_steps = offsets(seqs), offsets(pairs)
    meet(
        [{"seq": turn("seq", step)} for step in seq_steps]
        + [{"pair": turn("pair", step)} for step in pair_steps]
    )
    order = [(w, step) for w in range(count) for step in seq_steps + [0]]
    to_pair, to_seq = {}, {}
    for w, seq_step in order:
        for step in pair_steps:
            index = (step - 1) * seqs + seq_step
            target = turn("pair", step)
            copy = remote(
                parts[w].at[target * seqs + turn("seq", seq_step)],
                pair_in[w].at[index],
                pair_send.at[w, index],
                pair_recv.at[w, index],
                {"pair": target},
            )
            copy.start()
            to_pair[w, index] = copy
    for w, seq_step in order:
        total = parts[w][pair * seqs + turn("seq", seq_step)].astype(jnp.float32)
        for step in pair_steps:
            index = (step - 1) * seqs + seq_step
            to_pair[w, index].wait_recv()
            total = total + pair_in[w][index].astype(jnp.float32)
        if seq_step == 0:
            outs[w][...] = total
        else:
            seq_out[w][seq_step - 1] = total.astype(jnp.bfloat16)
            copy = remote(
                seq_out[w].at[seq_step - 1],
                seq_in[w].at[seq_step - 1],
                seq_send.at[w, seq_step - 1],
                seq_recv.at[w, seq_step - 1],
                {"seq": turn("seq", seq_step)},
            )
            copy.start()
            to_seq[w, seq_step] = copy
    for w in range(count):
        total = outs[w][...]
        for step in seq_steps:
            to_seq[w, step].wait_recv()
            total = total + seq_in[w][step - 1].astype(jnp.float32)
        outs[w][...] = total
    for copy in list(to_pair.values()) + list(to_seq.values()):
        copy.wait_send()


def scatter_all(parts):
    pairs, seqs = lax.axis_size("pair"), lax.axis_size("seq")
    count = len(parts)
    vmem = pl.BlockSpec(memory_space=pltpu.VMEM)
    dma = pltpu.SemaphoreType.DMA
    blocks = [x.shape[1:] for x in parts]
    from_pairs = (pairs - 1) * seqs
    return pl.pallas_call(
        functools.partial(scatter_kernel, pairs, seqs, count),
        out_shape=[jax.ShapeDtypeStruct(block, jnp.float32) for block in blocks],
        in_specs=[vmem] * count,
        out_specs=[vmem] * count,
        scratch_shapes=[pltpu.VMEM((from_pairs,) + block, jnp.bfloat16) for block in blocks]
        + [pltpu.VMEM((seqs - 1,) + block, jnp.bfloat16) for block in blocks] * 2
        + [
            dma((count, from_pairs)),
            dma((count, from_pairs)),
            dma((count, seqs - 1)),
            dma((count, seqs - 1)),
        ],
        compiler_params=pltpu.CompilerParams(
            collective_id=2, has_side_effects=True, vmem_limit_bytes=40 * 2**20
        ),
        name="scatter_grads",
    )(*parts)


def my_half(columns):
    pairs = lax.axis_size("pair")
    rows, width = columns.shape
    view = columns.reshape(rows, pairs, 2, width // (2 * pairs))
    mine = lax.dynamic_index_in_dim(view, lax.axis_index("core"), 2, keepdims=False)
    return mine.reshape(rows, width // 2)


def on_device(
    ends_in, clip_counts, qkv_weight, out_weight, up_weight, down_weight, norm_gains, vec_bias, up_bias
):
    ends_local = ends_in[0]
    batches, local_clips, frames, width = ends_local.shape
    clips = batches * local_clips
    rows = clips * frames
    owners = lax.axis_size("pair") * 2 * lax.axis_size("seq")
    share = width // owners
    ff_share = up_bias.shape[1]
    small = jnp.concatenate([norm_gains[0], vec_bias[0]], axis=0).reshape(-1)
    small = jnp.concatenate([small, up_bias[0]])
    extra = -(-small.shape[0] // width)
    extra_rows = -(-extra // 16) * 16
    small = jnp.pad(small, (0, extra_rows * width - small.shape[0])).reshape(extra_rows, width)
    out_small = jnp.concatenate([out_weight[0], small], axis=0)
    qkv_full, out_small, up_full, down_full = gather_all(
        [qkv_weight[0], out_small, up_weight[0], down_weight[0]]
    )
    out_full = out_small[:, :share].reshape(width, width)
    small_full = out_small[:, share:].reshape(owners, extra_rows * width).astype(jnp.float32)
    rows8 = small_full[:, : 8 * share].reshape(owners, 8, share)
    rows8 = rows8.transpose(1, 0, 2).reshape(8, width)
    up_shift = small_full[:, 8 * share : 8 * share + ff_share].reshape(-1)
    weights = (
        qkv_full.reshape(width, -1),
        out_full,
        up_full.reshape(width, -1),
        down_full.reshape(-1, width),
        rows8[:2],
        rows8[2:],
        up_shift,
    )
    first = lax.axis_index("section") == 0
    ends_rows = ends_local.reshape(rows, width)
    passed, _ = layer_forward(ends_rows.astype(jnp.float32), clips, frames, weights)
    link = lax.ppermute(passed.astype(jnp.bfloat16), "section", [(0, 1)])
    layer_in = jnp.where(first, ends_rows, link).astype(jnp.float32)
    top, kept = layer_forward(layer_in, clips, frames, weights)

    clip_ids = (lax.axis_index("pair") * 2 + lax.axis_index("core")) * local_clips
    clip_ids = clip_ids + jnp.arange(local_clips, dtype=jnp.int32)
    valid = (clip_ids[None, :] < clip_counts[:, None]).astype(jnp.bfloat16)
    cotangent = (ends_local * valid[:, :, None, None]).reshape(rows, width)
    passed_g, _, _ = layer_backward(
        cotangent.astype(jnp.float32), clips, frames, kept, weights
    )
    link_g = lax.ppermute(passed_g.astype(jnp.bfloat16), "section", [(1, 0)])
    grad_in = jnp.where(first, link_g, cotangent).astype(jnp.float32)
    bottom, operands, sums = layer_backward(grad_in, clips, frames, kept, weights)

    def over_rows(index):
        return jnp.sum(operands[index], axis=0, dtype=jnp.float32)

    qkv_sum = over_rows(1)
    columns = jnp.stack(
        sums + [qkv_sum[:width], qkv_sum[2 * width :], over_rows(3), over_rows(7)]
    )
    small_g = jnp.concatenate(
        [
            columns.reshape(8, owners, share).transpose(1, 0, 2).reshape(owners, 8 * share),
            over_rows(5).reshape(owners, ff_share),
        ],
        axis=1,
    )
    spare = extra_rows * width - small_g.shape[1]
    small_g = jnp.pad(small_g, ((0, 0), (0, spare))).reshape(owners * extra_rows, width)
    *swapped, small_other = swap_cores(list(operands) + [small_g])
    small_half = lax.dynamic_index_in_dim(
        (small_g + small_other).reshape(lax.axis_size("pair"), 2, -1, width),
        lax.axis_index("core"),
        1,
        keepdims=False,
    ).reshape(owners // 2, extra_rows, width)

    def part_grad(index):
        left = jnp.concatenate([my_half(operands[index]), my_half(swapped[index])], axis=0)
        right = jnp.concatenate([operands[index + 1], swapped[index + 1]], axis=0)
        part = transposed_times(left, right).astype(jnp.bfloat16)
        return part.reshape(owners // 2, -1, part.shape[1])

    out_half = jnp.concatenate([part_grad(2), small_half.astype(jnp.bfloat16)], axis=1)
    qkv_part, out_part, up_part, down_part = scatter_all(
        [part_grad(0), out_half, part_grad(4), part_grad(6)]
    )
    small_part = out_part[share:].reshape(-1)
    rows_part = small_part[: 8 * share].reshape(8, share)
    ends_out = jnp.where(first, bottom, top).reshape(1, batches, local_clips, frames, width)
    return (
        ends_out,
        qkv_part[None],
        out_part[:share][None],
        up_part[None],
        down_part[None],
        rows_part[None, :2],
        rows_part[None, 2:],
        small_part[None, 8 * share : 8 * share + ff_share],
    )


def solution(mesh):
    sections, clips, seqs = mesh.devices.shape
    fine = Mesh(
        mesh.devices.reshape(sections, clips // 2, 2, seqs), ("section", "pair", "core", "seq")
    )
    spread = ("pair", "core", "seq")
    ends = P("section", None, ("pair", "core"), "seq", None)
    rowed = P("section", spread, None)
    lanes = P("section", None, spread)
    up_bias = P("section", spread)
    return jax.shard_map(
        on_device,
        mesh=fine,
        in_specs=(ends, P(), rowed, rowed, rowed, rowed, lanes, lanes, up_bias),
        out_specs=(ends, rowed, rowed, rowed, rowed, lanes, lanes, up_bias),
        check_vma=False,
    )
```

```python
import functools

import jax
import jax.numpy as jnp
from jax import lax
from jax.experimental import pallas as pl
from jax.experimental.pallas import tpu as pltpu
from jax.sharding import Mesh
from jax.sharding import PartitionSpec as P

HEAD_DIM = 64
SCALE = HEAD_DIM ** (-0.5)


def norm_parts(values):
    centered = values - jnp.mean(values, axis=-1, keepdims=True)
    inverse = lax.rsqrt(jnp.mean(centered * centered, axis=-1, keepdims=True) + 1e-05)
    return centered * inverse, inverse


def norm_back(grad_hat, normal, inverse):
    first_term = grad_hat - jnp.mean(grad_hat, axis=-1, keepdims=True)
    return inverse * (first_term - normal * jnp.mean(grad_hat * normal, axis=-1, keepdims=True))


def matmul(left, right):
    return jnp.dot(left, right, preferred_element_type=jnp.float32)


def times_transposed(left, right):
    return lax.dot_general(
        left, right, (((1,), (1,)), ((), ())), preferred_element_type=jnp.float32
    )


def transposed_times(left, right):
    return lax.dot_general(
        left, right, (((0,), (0,)), ((), ())), preferred_element_type=jnp.float32
    )


def product(spec, left, right):
    return jnp.einsum(spec, left, right, preferred_element_type=jnp.float32)


def exchange_kernel(peers, parts, got, own_sem, send, receive):
    me = lax.axis_index("seq")
    meet([{"seq": turn("seq", step)} for step in offsets(peers)])
    copies = []
    for step in offsets(peers):
        target = turn("seq", step)
        copy = remote(
            parts.at[target], got.at[me], send.at[step], receive.at[step], {"seq": target}
        )
        copy.start()
        copies.append(copy)
    local = pltpu.make_async_copy(parts.at[me], got.at[me], own_sem)
    local.start()
    local.wait()
    for copy in copies:
        copy.wait()


def exchange(parts):
    peers = parts.shape[0]
    vmem = pl.BlockSpec(memory_space=pltpu.VMEM)
    dma = pltpu.SemaphoreType.DMA
    return pl.pallas_call(
        functools.partial(exchange_kernel, peers),
        out_shape=jax.ShapeDtypeStruct(parts.shape, parts.dtype),
        in_specs=[vmem],
        out_specs=vmem,
        scratch_shapes=[dma, dma((peers,)), dma((peers,))],
        compiler_params=pltpu.CompilerParams(
            collective_id=3 if parts.shape[1] == 1 else 4,
            has_side_effects=True,
            vmem_limit_bytes=24 * 2**20,
        ),
        name="exchange_heads",
    )(parts)


def to_heads(rows, groups, clips, frames):
    peers = lax.axis_size("seq")
    own = rows.shape[1] // (groups * peers)
    parts = rows.reshape(clips, frames, groups, peers, own).transpose(3, 2, 1, 0, 4)
    got = exchange(parts.reshape(peers, groups, frames, clips * own))
    got = got.reshape(peers, groups, frames, clips, own).transpose(1, 3, 0, 2, 4)
    return got.reshape(groups, clips, peers * frames, own // HEAD_DIM, HEAD_DIM)


def from_heads(heads, groups, clips, frames):
    peers = lax.axis_size("seq")
    own = heads.shape[-1]
    parts = heads.reshape(groups, clips, peers, frames, own).transpose(2, 0, 3, 1, 4)
    got = exchange(parts.reshape(peers, groups, frames, clips * own))
    got = got.reshape(peers, groups, frames, clips, own).transpose(3, 2, 1, 0, 4)
    return got.reshape(clips * frames, groups * peers * own)


def layer_forward(row_data, clips, frames, weights):
    qkv_weight, out_weight, up_weight, down_weight, gain_rows, shifts, up_shift = weights
    width = row_data.shape[1]
    normal_one, inverse_one = norm_parts(row_data)
    normed_one = (normal_one * gain_rows[0] + shifts[0]).astype(jnp.bfloat16)
    qkv_shift = jnp.concatenate([shifts[2], jnp.zeros_like(shifts[2]), shifts[3]])
    projected = (matmul(normed_one, qkv_weight) + qkv_shift).astype(jnp.bfloat16)
    triple = to_heads(projected, 3, clips, frames)
    scores = product("nqhd,nkhd->nhqk", triple[0], triple[1]) * SCALE
    weights_exp = jnp.exp(scores - jnp.max(scores, axis=-1, keepdims=True))
    soft = weights_exp / jnp.sum(weights_exp, axis=-1, keepdims=True)
    probs = soft.astype(jnp.bfloat16)
    mixed_heads = product("nhqk,nkhd->nqhd", probs, triple[2]).astype(jnp.bfloat16)
    total = mixed_heads.shape[1]
    mixed_rows = from_heads(mixed_heads.reshape(1, clips, total, -1), 1, clips, frames)
    hidden = row_data + matmul(mixed_rows, out_weight) + shifts[4]
    normal_two, inverse_two = norm_parts(hidden)
    normed_two = (normal_two * gain_rows[1] + shifts[1]).astype(jnp.bfloat16)
    before = matmul(normed_two, up_weight) + up_shift
    half = 0.5 * (1.0 + lax.erf(before * (0.5**0.5)))
    activated = (before * half).astype(jnp.bfloat16)
    slope = half + before * jnp.exp(-0.5 * before * before) * 0.3989422804014327
    result = hidden + matmul(activated, down_weight) + shifts[5]
    kept = (
        normal_one,
        inverse_one,
        normed_one,
        triple,
        soft,
        probs,
        mixed_rows,
        normal_two,
        inverse_two,
        normed_two,
        slope,
        activated,
    )
    return result, kept


def layer_backward(grad_rows, clips, frames, kept, weights):
    qkv_weight, out_weight, up_weight, down_weight, gain_rows, shifts, up_shift = weights
    (
        normal_one,
        inverse_one,
        normed_one,
        triple,
        soft,
        probs,
        mixed_rows,
        normal_two,
        inverse_two,
        normed_two,
        slope,
        activated,
    ) = kept
    down_g = grad_rows.astype(jnp.bfloat16)
    up_g = (times_transposed(down_g, down_weight) * slope).astype(jnp.bfloat16)
    norm_two_g = times_transposed(up_g, up_weight)
    hidden_g = grad_rows + norm_back(norm_two_g * gain_rows[1], normal_two, inverse_two)
    branch_g = hidden_g.astype(jnp.bfloat16)
    mixed_g = times_transposed(branch_g, out_weight).astype(jnp.bfloat16)
    mixed_heads = to_heads(mixed_g, 1, clips, frames)[0]
    probs_g = product("nqhd,nkhd->nhqk", mixed_heads, triple[2])
    delta = jnp.sum(soft * probs_g, axis=-1, keepdims=True)
    scores_g = (soft * (probs_g - delta)).astype(jnp.bfloat16)
    query_g = product("nhqk,nkhd->nqhd", scores_g, triple[1]) * SCALE
    key_g = product("nhqk,nqhd->nkhd", scores_g, triple[0]) * SCALE
    value_g = product("nhqk,nqhd->nkhd", probs, mixed_heads)
    stacked = jnp.stack([query_g, key_g, value_g]).astype(jnp.bfloat16)
    total = stacked.shape[2]
    qkv_g = from_heads(stacked.reshape(3, clips, total, -1), 3, clips, frames)
    norm_one_g = times_transposed(qkv_g, qkv_weight)
    input_g = hidden_g + norm_back(norm_one_g * gain_rows[0], normal_one, inverse_one)
    operands = (normed_one, qkv_g, mixed_rows, branch_g, normed_two, up_g, activated, down_g)
    sums = [
        jnp.sum(norm_one_g * normal_one, axis=0),
        jnp.sum(norm_two_g * normal_two, axis=0),
        jnp.sum(norm_one_g, axis=0),
        jnp.sum(norm_two_g, axis=0),
    ]
    return input_g, operands, sums


def turn(axis, step):
    size = lax.axis_size(axis)
    return lax.rem(lax.axis_index(axis) + step, size)


def offsets(size):
    near = []
    for step in range(1, size // 2 + 1):
        near.append(step)
        if size - step != step:
            near.append(size - step)
    return near


def meet(partners):
    barrier = pltpu.get_barrier_semaphore()
    for partner in partners:
        pl.semaphore_signal(
            barrier, inc=1, device_id=partner, device_id_type=pl.DeviceIdType.MESH
        )
    pl.semaphore_wait(barrier, len(partners))


def remote(source, target, send, receive, device):
    return pltpu.make_async_remote_copy(
        src_ref=source,
        dst_ref=target,
        send_sem=send,
        recv_sem=receive,
        device_id=device,
        device_id_type=pl.DeviceIdType.MESH,
    )


def gather_kernel(pairs, seqs, count, *refs):
    shards, fulls = refs[:count], refs[count : 2 * count]
    own_sem, seq_send, pair_send, core_send, lane_recv, core_recv = refs[2 * count :]
    pair, core, seq = (lax.axis_index(name) for name in ("pair", "core", "seq"))
    other = {"core": 1 - core}
    seq_steps, pair_steps = offsets(seqs), offsets(pairs)
    meet(
        [{"seq": turn("seq", step)} for step in seq_steps]
        + [{"pair": turn("pair", step)} for step in pair_steps]
        + [other]
    )

    def slot(pair_index, core_index, seq_index):
        return (pair_index * 2 + core_index) * seqs + seq_index

    started, waits = [], []

    def start(copy):
        copy.start()
        started.append(copy)

    def to_core(w, source, place, index):
        start(
            remote(
                source, fulls[w].at[place], core_send.at[w, index], core_recv.at[w, index], other
            )
        )

    def to_pairs(w, source, place, seq_step):
        for step in pair_steps:
            index = step * seqs + seq_step
            start(
                remote(
                    source,
                    fulls[w].at[place],
                    pair_send.at[w, index],
                    lane_recv.at[w, index],
                    {"pair": turn("pair", step)},
                )
            )

    mine = slot(pair, core, seq)
    local = []
    for w in range(count):
        for step in seq_steps:
            start(
                remote(
                    shards[w],
                    fulls[w].at[mine],
                    seq_send.at[w, step],
                    lane_recv.at[w, step],
                    {"seq": turn("seq", step)},
                )
            )
        to_pairs(w, shards[w], mine, 0)
        to_core(w, shards[w], mine, 0)
        copy = pltpu.make_async_copy(shards[w], fulls[w].at[mine], own_sem.at[w])
        copy.start()
        local.append(copy)

    def arrived(w, place, index, semaphores):
        there = fulls[w].at[place]
        remote(there, there, core_send.at[w, index], semaphores.at[w, index], other).wait_recv()

    for w in range(count):
        for step in seq_steps:
            place = slot(pair, core, turn("seq", seqs - step))
            arrived(w, place, step, lane_recv)
            to_pairs(w, fulls[w].at[place], place, step)
            to_core(w, fulls[w].at[place], place, step)
        for seq_step in [0] + seq_steps:
            for step in pair_steps:
                place = slot(
                    turn("pair", pairs - step), core, turn("seq", seqs - seq_step)
                )
                index = step * seqs + seq_step
                arrived(w, place, index, lane_recv)
                to_core(w, fulls[w].at[place], place, index)
    for w in range(count):
        for seq_step in range(seqs):
            for step in range(pairs):
                place = slot(
                    turn("pair", pairs - step), 1 - core, turn("seq", seqs - seq_step)
                )
                arrived(w, place, step * seqs + seq_step, core_recv)
    for copy in started:
        copy.wait_send()
    for copy in local:
        copy.wait()


def gather_all(shards):
    pairs, seqs = lax.axis_size("pair"), lax.axis_size("seq")
    count, lanes = len(shards), pairs * seqs
    dma = pltpu.SemaphoreType.DMA
    anywhere = pl.BlockSpec(memory_space=pl.ANY)
    return pl.pallas_call(
        functools.partial(gather_kernel, pairs, seqs, count),
        out_shape=[jax.ShapeDtypeStruct((2 * lanes,) + x.shape, x.dtype) for x in shards],
        in_specs=[anywhere] * count,
        out_specs=[anywhere] * count,
        scratch_shapes=[
            dma((count,)),
            dma((count, seqs)),
            dma((count, lanes)),
            dma((count, lanes)),
            dma((count, lanes)),
            dma((count, lanes)),
        ],
        compiler_params=pltpu.CompilerParams(collective_id=0, has_side_effects=True),
        name="gather_weights",
    )(*shards)


def swap_kernel(count, *refs):
    sources, targets = refs[:count], refs[count : 2 * count]
    send, receive = refs[2 * count :]
    other = {"core": 1 - lax.axis_index("core")}
    meet([other])
    copies = [
        remote(sources[i], targets[i], send.at[i], receive.at[i], other) for i in range(count)
    ]
    for copy in copies:
        copy.start()
    for copy in copies:
        copy.wait()


def swap_cores(arrays):
    count = len(arrays)
    vmem = pl.BlockSpec(memory_space=pltpu.VMEM)
    return pl.pallas_call(
        functools.partial(swap_kernel, count),
        out_shape=[jax.ShapeDtypeStruct(x.shape, x.dtype) for x in arrays],
        in_specs=[vmem] * count,
        out_specs=[vmem] * count,
        scratch_shapes=[pltpu.SemaphoreType.DMA((count,)), pltpu.SemaphoreType.DMA((count,))],
        compiler_params=pltpu.CompilerParams(
            collective_id=1, has_side_effects=True, vmem_limit_bytes=24 * 2**20
        ),
        name="swap_cores",
    )(*arrays)


def scatter_kernel(pairs, seqs, count, *refs):
    parts, outs = refs[:count], refs[count : 2 * count]
    pair_in = refs[2 * count : 3 * count]
    seq_out = refs[3 * count : 4 * count]
    seq_in = refs[4 * count : 5 * count]
    pair_send, pair_recv, seq_send, seq_recv = refs[5 * count :]
    pair = lax.axis_index("pair")
    seq_steps, pair_steps = offsets(seqs), offsets(pairs)
    meet(
        [{"seq": turn("seq", step)} for step in seq_steps]
        + [{"pair": turn("pair", step)} for step in pair_steps]
    )
    order = [(w, step) for w in range(count) for step in seq_steps + [0]]
    to_pair, to_seq = {}, {}
    for w, seq_step in order:
        for step in pair_steps:
            index = (step - 1) * seqs + seq_step
            target = turn("pair", step)
            copy = remote(
                parts[w].at[target * seqs + turn("seq", seq_step)],
                pair_in[w].at[index],
                pair_send.at[w, index],
                pair_recv.at[w, index],
                {"pair": target},
            )
            copy.start()
            to_pair[w, index] = copy
    for w, seq_step in order:
        total = parts[w][pair * seqs + turn("seq", seq_step)].astype(jnp.float32)
        for step in pair_steps:
            index = (step - 1) * seqs + seq_step
            to_pair[w, index].wait_recv()
            total = total + pair_in[w][index].astype(jnp.float32)
        if seq_step == 0:
            outs[w][...] = total
        else:
            seq_out[w][seq_step - 1] = total.astype(jnp.bfloat16)
            copy = remote(
                seq_out[w].at[seq_step - 1],
                seq_in[w].at[seq_step - 1],
                seq_send.at[w, seq_step - 1],
                seq_recv.at[w, seq_step - 1],
                {"seq": turn("seq", seq_step)},
            )
            copy.start()
            to_seq[w, seq_step] = copy
    for w in range(count):
        total = outs[w][...]
        for step in seq_steps:
            to_seq[w, step].wait_recv()
            total = total + seq_in[w][step - 1].astype(jnp.float32)
        outs[w][...] = total
    for copy in list(to_pair.values()) + list(to_seq.values()):
        copy.wait_send()


def scatter_all(parts):
    pairs, seqs = lax.axis_size("pair"), lax.axis_size("seq")
    count = len(parts)
    vmem = pl.BlockSpec(memory_space=pltpu.VMEM)
    dma = pltpu.SemaphoreType.DMA
    blocks = [x.shape[1:] for x in parts]
    from_pairs = (pairs - 1) * seqs
    return pl.pallas_call(
        functools.partial(scatter_kernel, pairs, seqs, count),
        out_shape=[jax.ShapeDtypeStruct(block, jnp.float32) for block in blocks],
        in_specs=[vmem] * count,
        out_specs=[vmem] * count,
        scratch_shapes=[pltpu.VMEM((from_pairs,) + block, jnp.bfloat16) for block in blocks]
        + [pltpu.VMEM((seqs - 1,) + block, jnp.bfloat16) for block in blocks] * 2
        + [
            dma((count, from_pairs)),
            dma((count, from_pairs)),
            dma((count, seqs - 1)),
            dma((count, seqs - 1)),
        ],
        compiler_params=pltpu.CompilerParams(
            collective_id=2, has_side_effects=True, vmem_limit_bytes=40 * 2**20
        ),
        name="scatter_grads",
    )(*parts)


def my_half(columns):
    pairs = lax.axis_size("pair")
    block = columns.shape[1] // (2 * pairs)
    even = lax.axis_index("core") == 0
    halves = [
        jnp.where(
            even,
            columns[:, 2 * i * block : (2 * i + 1) * block],
            columns[:, (2 * i + 1) * block : (2 * i + 2) * block],
        )
        for i in range(pairs)
    ]
    return jnp.concatenate(halves, axis=1)


def on_device(
    ends_in, clip_counts, qkv_weight, out_weight, up_weight, down_weight, norm_gains, vec_bias, up_bias
):
    ends_local = ends_in[0]
    batches, local_clips, frames, width = ends_local.shape
    clips = batches * local_clips
    rows = clips * frames
    owners = lax.axis_size("pair") * 2 * lax.axis_size("seq")
    share = width // owners
    ff_share = up_bias.shape[1]
    small = jnp.concatenate([norm_gains[0], vec_bias[0]], axis=0).reshape(-1)
    small = jnp.concatenate([small, up_bias[0]])
    extra = -(-small.shape[0] // width)
    extra_rows = -(-extra // 16) * 16
    small = jnp.pad(small, (0, extra_rows * width - small.shape[0])).reshape(extra_rows, width)
    out_small = jnp.concatenate([out_weight[0], small], axis=0)
    qkv_full, out_small, up_full, down_full = gather_all(
        [qkv_weight[0], out_small, up_weight[0], down_weight[0]]
    )
    out_full = out_small[:, :share].reshape(width, width)
    small_full = out_small[:, share:].reshape(owners, extra_rows * width).astype(jnp.float32)
    rows8 = small_full[:, : 8 * share].reshape(owners, 8, share)
    rows8 = rows8.transpose(1, 0, 2).reshape(8, width)
    up_shift = small_full[:, 8 * share : 8 * share + ff_share].reshape(-1)
    weights = (
        qkv_full.reshape(width, -1),
        out_full,
        up_full.reshape(width, -1),
        down_full.reshape(-1, width),
        rows8[:2],
        rows8[2:],
        up_shift,
    )
    first = lax.axis_index("section") == 0
    ends_rows = ends_local.reshape(rows, width)
    passed, _ = layer_forward(ends_rows.astype(jnp.float32), clips, frames, weights)
    link = lax.ppermute(passed.astype(jnp.bfloat16), "section", [(0, 1)])
    layer_in = jnp.where(first, ends_rows, link).astype(jnp.float32)
    top, kept = layer_forward(layer_in, clips, frames, weights)

    clip_ids = (lax.axis_index("pair") * 2 + lax.axis_index("core")) * local_clips
    clip_ids = clip_ids + jnp.arange(local_clips, dtype=jnp.int32)
    valid = (clip_ids[None, :] < clip_counts[:, None]).astype(jnp.bfloat16)
    cotangent = (ends_local * valid[:, :, None, None]).reshape(rows, width)
    passed_g, _, _ = layer_backward(
        cotangent.astype(jnp.float32), clips, frames, kept, weights
    )
    link_g = lax.ppermute(passed_g.astype(jnp.bfloat16), "section", [(1, 0)])
    grad_in = jnp.where(first, link_g, cotangent).astype(jnp.float32)
    bottom, operands, sums = layer_backward(grad_in, clips, frames, kept, weights)

    def over_rows(index):
        return jnp.sum(operands[index], axis=0, dtype=jnp.float32)

    qkv_sum = over_rows(1)
    columns = jnp.stack(
        sums + [qkv_sum[:width], qkv_sum[2 * width :], over_rows(3), over_rows(7)]
    )
    small_g = jnp.concatenate(
        [
            columns.reshape(8, owners, share).transpose(1, 0, 2).reshape(owners, 8 * share),
            over_rows(5).reshape(owners, ff_share),
        ],
        axis=1,
    )
    spare = extra_rows * width - small_g.shape[1]
    small_g = jnp.pad(small_g, ((0, 0), (0, spare))).reshape(owners * extra_rows, width)
    *swapped, small_other = swap_cores(list(operands) + [small_g])
    small_half = lax.dynamic_index_in_dim(
        (small_g + small_other).reshape(lax.axis_size("pair"), 2, -1, width),
        lax.axis_index("core"),
        1,
        keepdims=False,
    ).reshape(owners // 2, extra_rows, width)

    def part_grad(index):
        left = jnp.concatenate([my_half(operands[index]), my_half(swapped[index])], axis=0)
        right = jnp.concatenate([operands[index + 1], swapped[index + 1]], axis=0)
        part = transposed_times(left, right).astype(jnp.bfloat16)
        return part.reshape(owners // 2, -1, part.shape[1])

    out_half = jnp.concatenate([part_grad(2), small_half.astype(jnp.bfloat16)], axis=1)
    qkv_part, out_part, up_part, down_part = scatter_all(
        [part_grad(0), out_half, part_grad(4), part_grad(6)]
    )
    small_part = out_part[share:].reshape(-1)
    rows_part = small_part[: 8 * share].reshape(8, share)
    ends_out = jnp.where(first, bottom, top).reshape(1, batches, local_clips, frames, width)
    return (
        ends_out,
        qkv_part[None],
        out_part[:share][None],
        up_part[None],
        down_part[None],
        rows_part[None, :2],
        rows_part[None, 2:],
        small_part[None, 8 * share : 8 * share + ff_share],
    )


def solution(mesh):
    sections, clips, seqs = mesh.devices.shape
    fine = Mesh(
        mesh.devices.reshape(sections, clips // 2, 2, seqs), ("section", "pair", "core", "seq")
    )
    spread = ("pair", "core", "seq")
    ends = P("section", None, ("pair", "core"), "seq", None)
    rowed = P("section", spread, None)
    lanes = P("section", None, spread)
    up_bias = P("section", spread)
    return jax.shard_map(
        on_device,
        mesh=fine,
        in_specs=(ends, P(), rowed, rowed, rowed, rowed, lanes, lanes, up_bias),
        out_specs=(ends, rowed, rowed, rowed, rowed, lanes, lanes, up_bias),
        check_vma=False,
    )
```

```python
import functools

import jax
import jax.numpy as jnp
from jax import lax
from jax.experimental import pallas as pl
from jax.experimental.pallas import tpu as pltpu
from jax.sharding import Mesh
from jax.sharding import PartitionSpec as P

HEAD_DIM = 64
SCALE = HEAD_DIM ** (-0.5)


def norm_parts(values):
    centered = values - jnp.mean(values, axis=-1, keepdims=True)
    inverse = lax.rsqrt(jnp.mean(centered * centered, axis=-1, keepdims=True) + 1e-05)
    return centered * inverse, inverse


def norm_back(grad_hat, normal, inverse):
    first_term = grad_hat - jnp.mean(grad_hat, axis=-1, keepdims=True)
    return inverse * (first_term - normal * jnp.mean(grad_hat * normal, axis=-1, keepdims=True))


def matmul(left, right):
    return jnp.dot(left, right, preferred_element_type=jnp.float32)


def times_transposed(left, right):
    return lax.dot_general(
        left, right, (((1,), (1,)), ((), ())), preferred_element_type=jnp.float32
    )


def transposed_times(left, right):
    return lax.dot_general(
        left, right, (((0,), (0,)), ((), ())), preferred_element_type=jnp.float32
    )


def product(spec, left, right):
    return jnp.einsum(spec, left, right, preferred_element_type=jnp.float32)


def exchange_kernel(peers, parts, got, own_sem, send, receive):
    me = lax.axis_index("seq")
    meet([{"seq": turn("seq", step)} for step in offsets(peers)])
    copies = []
    for step in offsets(peers):
        target = turn("seq", step)
        copy = remote(
            parts.at[target], got.at[me], send.at[step], receive.at[step], {"seq": target}
        )
        copy.start()
        copies.append(copy)
    local = pltpu.make_async_copy(parts.at[me], got.at[me], own_sem)
    local.start()
    local.wait()
    for copy in copies:
        copy.wait()


def exchange(parts):
    peers = parts.shape[0]
    vmem = pl.BlockSpec(memory_space=pltpu.VMEM)
    dma = pltpu.SemaphoreType.DMA
    return pl.pallas_call(
        functools.partial(exchange_kernel, peers),
        out_shape=jax.ShapeDtypeStruct(parts.shape, parts.dtype),
        in_specs=[vmem],
        out_specs=vmem,
        scratch_shapes=[dma, dma((peers,)), dma((peers,))],
        compiler_params=pltpu.CompilerParams(
            collective_id=3 if parts.shape[1] == 1 else 4,
            has_side_effects=True,
            vmem_limit_bytes=24 * 2**20,
        ),
        name="exchange_heads",
    )(parts)


def to_heads(rows, groups, clips, frames):
    peers = lax.axis_size("seq")
    own = rows.shape[1] // (groups * peers)
    parts = rows.reshape(clips, frames, groups, peers, own).transpose(3, 2, 1, 0, 4)
    got = exchange(parts.reshape(peers, groups, frames, clips * own))
    got = got.reshape(peers, groups, frames, clips, own).transpose(1, 3, 0, 2, 4)
    return got.reshape(groups, clips, peers * frames, own // HEAD_DIM, HEAD_DIM)


def from_heads(heads, groups, clips, frames):
    peers = lax.axis_size("seq")
    own = heads.shape[-1]
    parts = heads.reshape(groups, clips, peers, frames, own).transpose(2, 0, 3, 1, 4)
    got = exchange(parts.reshape(peers, groups, frames, clips * own))
    got = got.reshape(peers, groups, frames, clips, own).transpose(3, 2, 1, 0, 4)
    return got.reshape(clips * frames, groups * peers * own)


def layer_forward(row_data, clips, frames, weights):
    qkv_weight, out_weight, up_weight, down_weight, gain_rows, shifts, up_shift = weights
    width = row_data.shape[1]
    normal_one, inverse_one = norm_parts(row_data)
    normed_one = (normal_one * gain_rows[0] + shifts[0]).astype(jnp.bfloat16)
    qkv_shift = jnp.concatenate([shifts[2], jnp.zeros_like(shifts[2]), shifts[3]])
    projected = (matmul(normed_one, qkv_weight) + qkv_shift).astype(jnp.bfloat16)
    triple = to_heads(projected, 3, clips, frames)
    scores = product("nqhd,nkhd->nhqk", triple[0], triple[1]) * SCALE
    weights_exp = jnp.exp(scores - jnp.max(scores, axis=-1, keepdims=True))
    soft = weights_exp / jnp.sum(weights_exp, axis=-1, keepdims=True)
    probs = soft.astype(jnp.bfloat16)
    mixed_heads = product("nhqk,nkhd->nqhd", probs, triple[2]).astype(jnp.bfloat16)
    total = mixed_heads.shape[1]
    mixed_rows = from_heads(mixed_heads.reshape(1, clips, total, -1), 1, clips, frames)
    hidden = row_data + matmul(mixed_rows, out_weight) + shifts[4]
    normal_two, inverse_two = norm_parts(hidden)
    normed_two = (normal_two * gain_rows[1] + shifts[1]).astype(jnp.bfloat16)
    before = matmul(normed_two, up_weight) + up_shift
    half = 0.5 * (1.0 + lax.erf(before * (0.5**0.5)))
    activated = (before * half).astype(jnp.bfloat16)
    slope = half + before * jnp.exp(-0.5 * before * before) * 0.3989422804014327
    result = hidden + matmul(activated, down_weight) + shifts[5]
    kept = (
        normal_one,
        inverse_one,
        normed_one,
        triple,
        soft,
        probs,
        mixed_rows,
        normal_two,
        inverse_two,
        normed_two,
        slope,
        activated,
    )
    return result, kept


def layer_backward(grad_rows, clips, frames, kept, weights):
    qkv_weight, out_weight, up_weight, down_weight, gain_rows, shifts, up_shift = weights
    (
        normal_one,
        inverse_one,
        normed_one,
        triple,
        soft,
        probs,
        mixed_rows,
        normal_two,
        inverse_two,
        normed_two,
        slope,
        activated,
    ) = kept
    down_g = grad_rows.astype(jnp.bfloat16)
    up_g = (times_transposed(down_g, down_weight) * slope).astype(jnp.bfloat16)
    norm_two_g = times_transposed(up_g, up_weight)
    hidden_g = grad_rows + norm_back(norm_two_g * gain_rows[1], normal_two, inverse_two)
    branch_g = hidden_g.astype(jnp.bfloat16)
    mixed_g = times_transposed(branch_g, out_weight).astype(jnp.bfloat16)
    mixed_heads = to_heads(mixed_g, 1, clips, frames)[0]
    probs_g = product("nqhd,nkhd->nhqk", mixed_heads, triple[2])
    delta = jnp.sum(soft * probs_g, axis=-1, keepdims=True)
    scores_g = (soft * (probs_g - delta)).astype(jnp.bfloat16)
    query_g = product("nhqk,nkhd->nqhd", scores_g, triple[1]) * SCALE
    key_g = product("nhqk,nqhd->nkhd", scores_g, triple[0]) * SCALE
    value_g = product("nhqk,nqhd->nkhd", probs, mixed_heads)
    stacked = jnp.stack([query_g, key_g, value_g]).astype(jnp.bfloat16)
    total = stacked.shape[2]
    qkv_g = from_heads(stacked.reshape(3, clips, total, -1), 3, clips, frames)
    norm_one_g = times_transposed(qkv_g, qkv_weight)
    input_g = hidden_g + norm_back(norm_one_g * gain_rows[0], normal_one, inverse_one)
    operands = (normed_one, qkv_g, mixed_rows, branch_g, normed_two, up_g, activated, down_g)
    sums = [
        jnp.sum(norm_one_g * normal_one, axis=0),
        jnp.sum(norm_two_g * normal_two, axis=0),
        jnp.sum(norm_one_g, axis=0),
        jnp.sum(norm_two_g, axis=0),
    ]
    return input_g, operands, sums


def turn(axis, step):
    size = lax.axis_size(axis)
    return lax.rem(lax.axis_index(axis) + step, size)


def offsets(size):
    near = []
    for step in range(1, size // 2 + 1):
        near.append(step)
        if size - step != step:
            near.append(size - step)
    return near


def meet(partners):
    barrier = pltpu.get_barrier_semaphore()
    for partner in partners:
        pl.semaphore_signal(
            barrier, inc=1, device_id=partner, device_id_type=pl.DeviceIdType.MESH
        )
    pl.semaphore_wait(barrier, len(partners))


def remote(source, target, send, receive, device):
    return pltpu.make_async_remote_copy(
        src_ref=source,
        dst_ref=target,
        send_sem=send,
        recv_sem=receive,
        device_id=device,
        device_id_type=pl.DeviceIdType.MESH,
    )


def gather_kernel(pairs, seqs, count, *refs):
    shards, fulls = refs[:count], refs[count : 2 * count]
    own_sem, seq_send, pair_send, core_send, lane_recv, core_recv = refs[2 * count :]
    pair, core, seq = (lax.axis_index(name) for name in ("pair", "core", "seq"))
    other = {"core": 1 - core}
    seq_steps, pair_steps = offsets(seqs), offsets(pairs)
    meet(
        [{"seq": turn("seq", step)} for step in seq_steps]
        + [{"pair": turn("pair", step)} for step in pair_steps]
        + [other]
    )

    def slot(pair_index, core_index, seq_index):
        return (pair_index * 2 + core_index) * seqs + seq_index

    started, waits = [], []

    def start(copy):
        copy.start()
        started.append(copy)

    def to_core(w, source, place, index):
        start(
            remote(
                source, fulls[w].at[place], core_send.at[w, index], core_recv.at[w, index], other
            )
        )

    def to_pairs(w, source, place, seq_step):
        for step in pair_steps:
            index = step * seqs + seq_step
            start(
                remote(
                    source,
                    fulls[w].at[place],
                    pair_send.at[w, index],
                    lane_recv.at[w, index],
                    {"pair": turn("pair", step)},
                )
            )

    mine = slot(pair, core, seq)
    local = []
    for w in range(count):
        for step in seq_steps:
            start(
                remote(
                    shards[w],
                    fulls[w].at[mine],
                    seq_send.at[w, step],
                    lane_recv.at[w, step],
                    {"seq": turn("seq", step)},
                )
            )
        to_pairs(w, shards[w], mine, 0)
        to_core(w, shards[w], mine, 0)
        copy = pltpu.make_async_copy(shards[w], fulls[w].at[mine], own_sem.at[w])
        copy.start()
        local.append(copy)

    def arrived(w, place, index, semaphores):
        there = fulls[w].at[place]
        remote(there, there, core_send.at[w, index], semaphores.at[w, index], other).wait_recv()

    def from_seq(w):
        for step in seq_steps:
            place = slot(pair, core, turn("seq", seqs - step))
            arrived(w, place, step, lane_recv)
            to_pairs(w, fulls[w].at[place], place, step)
            to_core(w, fulls[w].at[place], place, step)

    def from_pairs(w):
        for seq_step in [0] + seq_steps:
            for step in pair_steps:
                place = slot(turn("pair", pairs - step), core, turn("seq", seqs - seq_step))
                index = step * seqs + seq_step
                arrived(w, place, index, lane_recv)
                to_core(w, fulls[w].at[place], place, index)

    from_seq(0)
    for w in range(1, count):
        from_seq(w)
        from_pairs(w - 1)
    from_pairs(count - 1)
    for w in range(count):
        for seq_step in range(seqs):
            for step in range(pairs):
                place = slot(
                    turn("pair", pairs - step), 1 - core, turn("seq", seqs - seq_step)
                )
                arrived(w, place, step * seqs + seq_step, core_recv)
    for copy in started:
        copy.wait_send()
    for copy in local:
        copy.wait()


def gather_all(shards):
    pairs, seqs = lax.axis_size("pair"), lax.axis_size("seq")
    count, lanes = len(shards), pairs * seqs
    dma = pltpu.SemaphoreType.DMA
    anywhere = pl.BlockSpec(memory_space=pl.ANY)
    return pl.pallas_call(
        functools.partial(gather_kernel, pairs, seqs, count),
        out_shape=[jax.ShapeDtypeStruct((2 * lanes,) + x.shape, x.dtype) for x in shards],
        in_specs=[anywhere] * count,
        out_specs=[anywhere] * count,
        scratch_shapes=[
            dma((count,)),
            dma((count, seqs)),
            dma((count, lanes)),
            dma((count, lanes)),
            dma((count, lanes)),
            dma((count, lanes)),
        ],
        compiler_params=pltpu.CompilerParams(collective_id=0, has_side_effects=True),
        name="gather_weights",
    )(*shards)


def swap_kernel(count, *refs):
    sources, targets = refs[:count], refs[count : 2 * count]
    send, receive = refs[2 * count :]
    other = {"core": 1 - lax.axis_index("core")}
    meet([other])
    copies = [
        remote(sources[i], targets[i], send.at[i], receive.at[i], other) for i in range(count)
    ]
    for copy in copies:
        copy.start()
    for copy in copies:
        copy.wait()


def swap_cores(arrays):
    count = len(arrays)
    vmem = pl.BlockSpec(memory_space=pltpu.VMEM)
    return pl.pallas_call(
        functools.partial(swap_kernel, count),
        out_shape=[jax.ShapeDtypeStruct(x.shape, x.dtype) for x in arrays],
        in_specs=[vmem] * count,
        out_specs=[vmem] * count,
        scratch_shapes=[pltpu.SemaphoreType.DMA((count,)), pltpu.SemaphoreType.DMA((count,))],
        compiler_params=pltpu.CompilerParams(
            collective_id=1, has_side_effects=True, vmem_limit_bytes=24 * 2**20
        ),
        name="swap_cores",
    )(*arrays)


def scatter_kernel(pairs, seqs, count, *refs):
    parts, outs = refs[:count], refs[count : 2 * count]
    pair_in = refs[2 * count : 3 * count]
    seq_out = refs[3 * count : 4 * count]
    seq_in = refs[4 * count : 5 * count]
    pair_send, pair_recv, seq_send, seq_recv = refs[5 * count :]
    pair = lax.axis_index("pair")
    seq_steps, pair_steps = offsets(seqs), offsets(pairs)
    meet(
        [{"seq": turn("seq", step)} for step in seq_steps]
        + [{"pair": turn("pair", step)} for step in pair_steps]
    )
    order = [(w, step) for w in range(count) for step in seq_steps + [0]]
    to_pair, to_seq = {}, {}
    for w, seq_step in order:
        for step in pair_steps:
            index = (step - 1) * seqs + seq_step
            target = turn("pair", step)
            copy = remote(
                parts[w].at[target * seqs + turn("seq", seq_step)],
                pair_in[w].at[index],
                pair_send.at[w, index],
                pair_recv.at[w, index],
                {"pair": target},
            )
            copy.start()
            to_pair[w, index] = copy
    for w, seq_step in order:
        total = parts[w][pair * seqs + turn("seq", seq_step)].astype(jnp.float32)
        for step in pair_steps:
            index = (step - 1) * seqs + seq_step
            to_pair[w, index].wait_recv()
            total = total + pair_in[w][index].astype(jnp.float32)
        if seq_step == 0:
            outs[w][...] = total
        else:
            seq_out[w][seq_step - 1] = total.astype(jnp.bfloat16)
            copy = remote(
                seq_out[w].at[seq_step - 1],
                seq_in[w].at[seq_step - 1],
                seq_send.at[w, seq_step - 1],
                seq_recv.at[w, seq_step - 1],
                {"seq": turn("seq", seq_step)},
            )
            copy.start()
            to_seq[w, seq_step] = copy
    for w in range(count):
        total = outs[w][...]
        for step in seq_steps:
            to_seq[w, step].wait_recv()
            total = total + seq_in[w][step - 1].astype(jnp.float32)
        outs[w][...] = total
    for copy in list(to_pair.values()) + list(to_seq.values()):
        copy.wait_send()


def scatter_all(parts):
    pairs, seqs = lax.axis_size("pair"), lax.axis_size("seq")
    count = len(parts)
    vmem = pl.BlockSpec(memory_space=pltpu.VMEM)
    dma = pltpu.SemaphoreType.DMA
    blocks = [x.shape[1:] for x in parts]
    from_pairs = (pairs - 1) * seqs
    return pl.pallas_call(
        functools.partial(scatter_kernel, pairs, seqs, count),
        out_shape=[jax.ShapeDtypeStruct(block, jnp.float32) for block in blocks],
        in_specs=[vmem] * count,
        out_specs=[vmem] * count,
        scratch_shapes=[pltpu.VMEM((from_pairs,) + block, jnp.bfloat16) for block in blocks]
        + [pltpu.VMEM((seqs - 1,) + block, jnp.bfloat16) for block in blocks] * 2
        + [
            dma((count, from_pairs)),
            dma((count, from_pairs)),
            dma((count, seqs - 1)),
            dma((count, seqs - 1)),
        ],
        compiler_params=pltpu.CompilerParams(
            collective_id=2, has_side_effects=True, vmem_limit_bytes=40 * 2**20
        ),
        name="scatter_grads",
    )(*parts)


def my_half(columns):
    pairs = lax.axis_size("pair")
    block = columns.shape[1] // (2 * pairs)
    even = lax.axis_index("core") == 0
    halves = [
        jnp.where(
            even,
            columns[:, 2 * i * block : (2 * i + 1) * block],
            columns[:, (2 * i + 1) * block : (2 * i + 2) * block],
        )
        for i in range(pairs)
    ]
    return jnp.concatenate(halves, axis=1)


def on_device(
    ends_in, clip_counts, qkv_weight, out_weight, up_weight, down_weight, norm_gains, vec_bias, up_bias
):
    ends_local = ends_in[0]
    batches, local_clips, frames, width = ends_local.shape
    clips = batches * local_clips
    rows = clips * frames
    owners = lax.axis_size("pair") * 2 * lax.axis_size("seq")
    share = width // owners
    ff_share = up_bias.shape[1]
    small = jnp.concatenate([norm_gains[0], vec_bias[0]], axis=0).reshape(-1)
    small = jnp.concatenate([small, up_bias[0]])
    extra = -(-small.shape[0] // width)
    extra_rows = -(-extra // 16) * 16
    small = jnp.pad(small, (0, extra_rows * width - small.shape[0])).reshape(extra_rows, width)
    up_full, down_full, qkv_full, out_full, small_full = gather_all(
        [up_weight[0], down_weight[0], qkv_weight[0], out_weight[0], small]
    )
    small_full = small_full.reshape(owners, extra_rows * width).astype(jnp.float32)
    rows8 = small_full[:, : 8 * share].reshape(owners, 8, share)
    rows8 = rows8.transpose(1, 0, 2).reshape(8, width)
    up_shift = small_full[:, 8 * share : 8 * share + ff_share].reshape(-1)
    weights = (
        qkv_full.reshape(width, -1),
        out_full.reshape(width, width),
        up_full.reshape(width, -1),
        down_full.reshape(-1, width),
        rows8[:2],
        rows8[2:],
        up_shift,
    )
    first = lax.axis_index("section") == 0
    ends_rows = ends_local.reshape(rows, width)
    passed, _ = layer_forward(ends_rows.astype(jnp.float32), clips, frames, weights)
    link = lax.ppermute(passed.astype(jnp.bfloat16), "section", [(0, 1)])
    layer_in = jnp.where(first, ends_rows, link).astype(jnp.float32)
    top, kept = layer_forward(layer_in, clips, frames, weights)

    clip_ids = (lax.axis_index("pair") * 2 + lax.axis_index("core")) * local_clips
    clip_ids = clip_ids + jnp.arange(local_clips, dtype=jnp.int32)
    valid = (clip_ids[None, :] < clip_counts[:, None]).astype(jnp.bfloat16)
    cotangent = (ends_local * valid[:, :, None, None]).reshape(rows, width)
    passed_g, _, _ = layer_backward(
        cotangent.astype(jnp.float32), clips, frames, kept, weights
    )
    link_g = lax.ppermute(passed_g.astype(jnp.bfloat16), "section", [(1, 0)])
    grad_in = jnp.where(first, link_g, cotangent).astype(jnp.float32)
    bottom, operands, sums = layer_backward(grad_in, clips, frames, kept, weights)

    def over_rows(index):
        return jnp.sum(operands[index], axis=0, dtype=jnp.float32)

    qkv_sum = over_rows(1)
    columns = jnp.stack(
        sums + [qkv_sum[:width], qkv_sum[2 * width :], over_rows(3), over_rows(7)]
    )
    small_g = jnp.concatenate(
        [
            columns.reshape(8, owners, share).transpose(1, 0, 2).reshape(owners, 8 * share),
            over_rows(5).reshape(owners, ff_share),
        ],
        axis=1,
    )
    spare = extra_rows * width - small_g.shape[1]
    small_g = jnp.pad(small_g, ((0, 0), (0, spare))).reshape(owners * extra_rows, width)
    *swapped, small_other = swap_cores(list(operands) + [small_g])
    small_half = lax.dynamic_index_in_dim(
        (small_g + small_other).reshape(lax.axis_size("pair"), 2, -1, width),
        lax.axis_index("core"),
        1,
        keepdims=False,
    ).reshape(owners // 2, extra_rows, width)

    def part_grad(index):
        left = jnp.concatenate([my_half(operands[index]), my_half(swapped[index])], axis=0)
        right = jnp.concatenate([operands[index + 1], swapped[index + 1]], axis=0)
        part = transposed_times(left, right).astype(jnp.bfloat16)
        return part.reshape(owners // 2, -1, part.shape[1])

    out_half = jnp.concatenate([part_grad(2), small_half.astype(jnp.bfloat16)], axis=1)
    up_part, down_part, qkv_part, out_part = scatter_all(
        [part_grad(4), part_grad(6), part_grad(0), out_half]
    )
    small_part = out_part[share:].reshape(-1)
    rows_part = small_part[: 8 * share].reshape(8, share)
    ends_out = jnp.where(first, bottom, top).reshape(1, batches, local_clips, frames, width)
    return (
        ends_out,
        qkv_part[None],
        out_part[:share][None],
        up_part[None],
        down_part[None],
        rows_part[None, :2],
        rows_part[None, 2:],
        small_part[None, 8 * share : 8 * share + ff_share],
    )


def solution(mesh):
    sections, clips, seqs = mesh.devices.shape
    fine = Mesh(
        mesh.devices.reshape(sections, clips // 2, 2, seqs), ("section", "pair", "core", "seq")
    )
    spread = ("pair", "core", "seq")
    ends = P("section", None, ("pair", "core"), "seq", None)
    rowed = P("section", spread, None)
    lanes = P("section", None, spread)
    up_bias = P("section", spread)
    return jax.shard_map(
        on_device,
        mesh=fine,
        in_specs=(ends, P(), rowed, rowed, rowed, rowed, lanes, lanes, up_bias),
        out_specs=(ends, rowed, rowed, rowed, rowed, lanes, lanes, up_bias),
        check_vma=False,
    )
```
